256 devices in a mesh: blk: 16 (over z, x_lo), fsdp: 16 (over x_hi, y, core).
Axes of the slice: x: 4 (x_hi: 2, x_lo: 2; x = x_hi * 2 + x_lo), y: 4, z: 8, core: 2. Of those that a mesh axis runs over, the one named last changes fastest.
Arguments:
- hidden: bfloat16 [32768, 6912], P(('blk', 'fsdp')), may hold values from -6 to 6
- residual: bfloat16 [16, 2560, 2048], P('blk', 'fsdp'), may hold values from -6 to 6
- cotangent: bfloat16 [16, 2560, 2048], P('blk', 'fsdp'), may hold values from -6 to 6
- weight: bfloat16 [16, 2560, 6912], P('blk', 'fsdp'), may hold values from -6 to 6
- self_sketch: float32 [16, 2560, 512], P('blk', 'fsdp'), may hold values from -6 to 6
- mix_sketch: float32 [16, 2560, 512], P('blk', 'fsdp'), may hold values from -6 to 6
- bucket: int32 [6912], replicated, may hold values from 0 to 511
- sign_bit: int32 [6912], replicated, may hold values from 0 to 1
Outputs:
- stream_out: bfloat16 [16, 2560, 2048], P('blk', 'fsdp')
- new_weight: bfloat16 [16, 2560, 6912], P('blk', 'fsdp')
- new_self: float32 [16, 2560, 512], P('blk', 'fsdp')
- new_mix: float32 [16, 2560, 512], P('blk', 'fsdp')
The draws below stay inside these ranges and needn't reach their ends.
All inputs are finite; a program needn't handle non-finite values.
Results may differ from the reference program's by a relative error of at most 0.007.
Values may be sent and summed in bfloat16 or wider, within the bound.
A program may use at most 256 MiB of HBM per device.

```python
import jax
import jax.numpy as jnp
from jax import lax

D = 2560
FF = 6912
SK = 512
TOKENS = 2048
N_BLK = 16


def plant(drawn, key, smallest, largest):
    longest = drawn.shape.index(max(drawn.shape))
    spots = []
    for shift in (0, 1):
        where = [jax.random.randint(jax.random.fold_in(key, axis), (), 0, length) for axis, length in enumerate(drawn.shape)]
        where[longest] = (where[longest] + shift) % drawn.shape[longest]
        spots.append(tuple(where))
    return drawn.at[spots[0]].set(smallest).at[spots[1]].set(largest)


def level_of(stream_key, shape, split, low, largest):
    def one(dim, blocks):
        steps = jax.random.uniform(jax.random.fold_in(jax.random.fold_in(stream_key, 6), dim), (blocks,), jnp.float32, low / len(split), largest / len(split))
        return jnp.repeat(jnp.exp(steps), shape[dim] // blocks).reshape((-1,) + (1,) * (len(shape) - dim - 1))

    level = one(*split[0])
    for cut in split[1:]:
        level = level * one(*cut)
    return level


def bell_draw(key, dims, scale, reach, pieces=(), kind=jnp.bfloat16):
    drawn = jax.random.normal(key, dims, jnp.float32) * scale
    if len(pieces) > 0:
        drawn = level_of(key, dims, pieces, -0.22, 0.18) * drawn
    return jnp.clip(drawn, min=-reach, max=reach).astype(kind)


def setup_inputs(seed: int = 0) -> dict:
    arg_keys = jax.random.split(jax.random.key(seed), 9)
    return {
        "hidden": bell_draw(arg_keys[0], (N_BLK * TOKENS, FF), 1.0, 6.0, ((0, 256),)),
        "residual": bell_draw(arg_keys[1], (N_BLK, D, TOKENS), 1.0, 6.0, ((0, 16), (1, 16))),
        "cotangent": bell_draw(arg_keys[2], (N_BLK, D, TOKENS), (max(1, FF // TOKENS) ** 0.5), 6.0, ((0, 16), (1, 16))),
        "weight": bell_draw(arg_keys[3], (N_BLK, D, FF), 1.0, 6.0, ((0, 16), (1, 16))),
        "self_sketch": bell_draw(arg_keys[4], (N_BLK, D, SK), 1.0, 6.0, ((0, 16), (1, 16)), jnp.float32),
        "mix_sketch": bell_draw(arg_keys[5], (N_BLK, D, SK), 1.0, 6.0, ((0, 16), (1, 16)), jnp.float32),
        "bucket": plant(jax.random.randint(arg_keys[6], (FF,), 0, SK), jax.random.fold_in(arg_keys[6], 1), 0, SK - 1).astype(jnp.int32),
        "sign_bit": plant(jax.random.randint(arg_keys[7], (FF,), 0, 2), jax.random.fold_in(arg_keys[7], 1), 0, 1).astype(jnp.int32),
    }


step_size = 0.3
consensus_rate = 0.5


def expand(sketch_rows, bucket, sign_values):
    return jnp.take(sketch_rows, bucket, axis=-1) * sign_values


def reference(hidden, residual, cotangent, weight, self_sketch, mix_sketch, bucket, sign_bit):
    sign_values = (2 * sign_bit - 1).astype(jnp.float32)
    sketch_table = (bucket[:, None] == jnp.arange(SK, dtype=jnp.int32)[None, :]).astype(jnp.float32) * sign_values[:, None]
    out_scale = FF ** -0.5
    sketch_ratio = SK / FF
    hidden_blocks = hidden.reshape(N_BLK, TOKENS, FF)

    def replica(inputs):
        hidden_rows, resid_rows, cotan_rows, weight_rows, own_sketch = inputs
        product = jnp.dot(weight_rows, hidden_rows.T, preferred_element_type=jnp.float32)
        stream = (resid_rows.astype(jnp.float32) + out_scale * product).astype(jnp.bfloat16)
        gradient = out_scale * jnp.dot(cotan_rows, hidden_rows, preferred_element_type=jnp.float32)
        stepped = weight_rows.astype(jnp.float32) - step_size * gradient
        change = stepped - expand(own_sketch, bucket, sign_values)
        sketched = sketch_ratio * jnp.dot(change, sketch_table, precision=lax.Precision.HIGHEST)
        return stream, stepped, sketched

    stream_out, stepped, sketched = lax.map(replica, (hidden_blocks, residual, cotangent, weight, self_sketch))
    from_left = jnp.roll(sketched, 1, axis=0)
    from_right = jnp.roll(sketched, -1, axis=0)
    new_self = self_sketch + sketched
    new_mix = mix_sketch + (from_left + sketched + from_right) / 3.0

    def update(inputs):
        stepped_rows, difference = inputs
        return (stepped_rows + consensus_rate * expand(difference, bucket, sign_values)).astype(jnp.bfloat16)

    new_weight = lax.map(update, (stepped, new_mix - new_self))
    return stream_out, new_weight, new_self, new_mix
```

```python
import functools

import jax
import jax.numpy as jnp
from jax import lax
from jax.experimental import pallas as pl
from jax.experimental.pallas import tpu as pltpu
from jax.sharding import PartitionSpec as P

MESH = pl.DeviceIdType.MESH
STEP_SIZE = 0.3
CONSENSUS = 0.5
CH = 256
LEAD = 4


def nt(a, b):
    return lax.dot_general(a, b, (((1,), (1,)), ((), ())), preferred_element_type=jnp.float32)


def nn(a, b):
    return jnp.dot(a, b, preferred_element_type=jnp.float32)


def kernel(
    hid, res, cot, wgt, slf, mix, bkt, sgn,
    out_s, out_w, out_self, out_mix,
    buf, wv, cv, rv, sv, mv, sacc, stepped, tbl, lhs, kacc, sk_send, sk_left, sk_right,
    lsem, insem, sem1, sem2, sem3, sibsem, ssem, xsem, osem,
):
    rows, ff = wgt.shape
    toks = hid.shape[0]
    nc = ff // CH
    nb, nf = lax.axis_size("blk"), lax.axis_size("fsdp")
    sk = slf.shape[1]
    blk, me = lax.axis_index("blk"), lax.axis_index("fsdp")
    xh, y, core = me // 8, (me // 2) % 4, me % 2
    xo = 1 - xh

    def at(a, b):
        return a * 8 + (b % 4) * 2 + core

    sibling = me + 1 - 2 * core
    up, down, across = at(xh, y + 1), at(xh, y + 3), at(xo, y)
    ahead, behind = (blk + 1) % nb, (blk + nb - 1) % nb

    def block(j, b):
        return buf.at[j, pl.ds(pl.multiple_of(b * toks, toks), toks), :]

    def columns(ref, j):
        return ref.at[:, pl.ds(pl.multiple_of(j * CH, CH), CH)]

    def load(j):
        return pltpu.make_async_copy(columns(hid, j), block(j, me), lsem.at[j])

    def send(j, b, to, recv, lane):
        pltpu.make_async_remote_copy(
            src_ref=block(j, b), dst_ref=block(j, b), send_sem=ssem.at[lane], recv_sem=recv.at[j],
            device_id=(blk, to), device_id_type=MESH,
        ).start()

    def arrived(j, sem, blocks):
        ref = buf.at[j, pl.ds(0, blocks * toks), :]
        pltpu.make_async_copy(ref, ref, sem.at[j]).wait()

    def own(j):
        load(j).wait()
        send(j, me, up, sem1, 0)
        send(j, me, down, sem1, 0)
        send(j, me, across, sem1, 0)
        send(j, me, sibling, sibsem, 1)

    def second(j):
        arrived(j, sem1, 3)
        kind = (j % 3) // 2
        turn = 1 + 2 * (j % 2)
        send(j, at(xh, y + 4 - turn), at(xh, y + turn), sem2, 0)
        send(j, (1 - kind) * across + kind * up, (1 - kind) * up + kind * across, sem2, 0)
        send(j, (1 - kind) * across + kind * down, (1 - kind) * down + kind * across, sem2, 0)
        send(j, up, sibling, sibsem, 1)
        send(j, down, sibling, sibsem, 1)
        send(j, across, sibling, sibsem, 1)

    def third(j):
        arrived(j, sem2, 3)
        kind = (j % 3) // 2
        turn = 1 + 2 * (1 - j % 2)
        send(
            j,
            (1 - kind) * at(xh, y + 2) + kind * at(xo, y + 4 - turn),
            (1 - kind) * across + kind * at(xh, y + turn),
            sem3,
            0,
        )
        send(j, at(xh, y + 2), sibling, sibsem, 1)
        send(j, at(xo, y + 1), sibling, sibsem, 1)
        send(j, at(xo, y + 3), sibling, sibsem, 1)

    def fourth(j):
        arrived(j, sem3, 1)
        send(j, at(xo, y + 2), sibling, sibsem, 1)

    def compute(j):
        arrived(j, sibsem, nf // 2)
        h = buf[j]
        cols = pl.ds(pl.multiple_of(j * CH, CH), CH)
        w = wv[:, cols]
        sacc[...] += nt(w, h)
        new = w.astype(jnp.float32) - (STEP_SIZE * ff**-0.5) * nn(cv[...], h)
        stepped[j] = new
        sign = (2 * sgn[:, cols] - 1).astype(jnp.float32)
        hot = lax.broadcasted_iota(jnp.int32, (sk, CH), 0) == bkt[:, cols]
        table = jnp.where(hot, jnp.broadcast_to(sign, (sk, CH)), 0.0).astype(jnp.bfloat16)
        tbl[j] = table
        high = new.astype(jnp.bfloat16)
        lhs[pl.ds(0, rows), :] = high
        lhs[pl.ds(rows, rows), :] = (new - high.astype(jnp.float32)).astype(jnp.bfloat16)
        lhs[pl.ds(2 * rows, 16), :] = jnp.broadcast_to(sign, (16, CH)).astype(jnp.bfloat16)
        kacc[...] += nt(lhs[...], table)

    for j in range(nc):
        load(j).start()
    ins = [(cot, cv), (wgt, wv), (res, rv), (slf, sv), (mix, mv)]
    ins = [pltpu.make_async_copy(a, b, insem.at[i]) for i, (a, b) in enumerate(ins)]
    for c in ins:
        c.start()
    barrier = pltpu.get_barrier_semaphore()
    for to in (up, down, across, sibling):
        pl.semaphore_signal(barrier, inc=1, device_id=(blk, to), device_id_type=MESH)
    for to in (ahead, behind):
        pl.semaphore_signal(barrier, inc=1, device_id=(to, me), device_id_type=MESH)
    pl.semaphore_wait(barrier, 6)

    def lead(j, c):
        own(j)
        return c

    lax.fori_loop(0, LEAD, lead, 0)
    sacc[...] = jnp.zeros_like(sacc)
    kacc[...] = jnp.zeros_like(kacc)
    for c in ins:
        c.wait()

    def step(i, c):
        @pl.when(i + LEAD < nc)
        def _():
            own(i + LEAD)

        @pl.when(i < nc)
        def _():
            second(i)

        @pl.when((i >= 1) & (i < nc + 1))
        def _():
            third(i - 1)

        @pl.when((i >= 2) & (i < nc + 2))
        def _():
            fourth(i - 2)

        @pl.when(i >= 3)
        def _():
            compute(i - 3)

        return c

    lax.fori_loop(0, nc + 3, step, 0)

    sketched = (sk / ff) * (
        kacc[pl.ds(0, rows), :] + kacc[pl.ds(rows, rows), :] - kacc[pl.ds(2 * rows, 1), :] * sv[...]
    )
    sk_send[...] = sketched.astype(jnp.bfloat16)
    swaps = [
        pltpu.make_async_remote_copy(
            src_ref=sk_send, dst_ref=dst, send_sem=xsem.at[2 * i], recv_sem=xsem.at[2 * i + 1],
            device_id=(to, me), device_id_type=MESH,
        )
        for i, (dst, to) in enumerate(((sk_left, ahead), (sk_right, behind)))
    ]
    for c in swaps:
        c.start()
    rv[...] = (rv[...].astype(jnp.float32) + (ff**-0.5) * sacc[...]).astype(jnp.bfloat16)
    outs = [pltpu.make_async_copy(rv, out_s, osem.at[0])]
    outs[0].start()
    sv[...] = sv[...] + sketched
    outs.append(pltpu.make_async_copy(sv, out_self, osem.at[1]))
    outs[1].start()
    mv[...] = mv[...] + sketched / 3.0
    for c in swaps:
        c.wait()
    mixed = mv[...] + (sk_left[...].astype(jnp.float32) + sk_right[...].astype(jnp.float32)) / 3.0
    mv[...] = mixed
    outs.append(pltpu.make_async_copy(mv, out_mix, osem.at[2]))
    outs[2].start()
    sk_send[...] = (CONSENSUS * (mixed - sv[...])).astype(jnp.bfloat16)

    def last(j, c):
        cols = pl.ds(pl.multiple_of(j * CH, CH), CH)
        wv[:, cols] = (stepped[j] + nn(sk_send[...], tbl[j])).astype(jnp.bfloat16)
        pltpu.make_async_copy(columns(wv, j), columns(out_w, j), osem.at[3]).start()
        return c

    lax.fori_loop(0, nc, last, 0)
    outs.append(pltpu.make_async_copy(wv, out_w, osem.at[3]))
    for c in outs:
        c.wait()
    for lane, blocks in ((0, 7), (1, 8)):
        ref = buf.at[:, pl.ds(0, blocks * toks), :]
        pltpu.make_async_copy(ref, ref, ssem.at[lane]).wait()


def body(hidden, residual, cotangent, weight, self_sketch, mix_sketch, bucket, sign_bit):
    toks, ff = hidden.shape
    _, rows, whole = residual.shape
    sk = self_sketch.shape[2]
    nc = ff // CH
    f32, bf16 = jnp.float32, jnp.bfloat16
    anywhere = pl.BlockSpec(memory_space=pl.ANY)
    vmem = pl.BlockSpec(memory_space=pltpu.VMEM)
    dma = pltpu.SemaphoreType.DMA
    outs = pl.pallas_call(
        kernel,
        out_shape=(
            jax.ShapeDtypeStruct((rows, whole), bf16),
            jax.ShapeDtypeStruct((rows, ff), bf16),
            jax.ShapeDtypeStruct((rows, sk), f32),
            jax.ShapeDtypeStruct((rows, sk), f32),
        ),
        in_specs=[anywhere] * 6 + [vmem] * 2,
        out_specs=(anywhere,) * 4,
        scratch_shapes=[
            pltpu.VMEM((nc, whole, CH), bf16),
            pltpu.VMEM((rows, ff), bf16),
            pltpu.VMEM((rows, whole), bf16),
            pltpu.VMEM((rows, whole), bf16),
            pltpu.VMEM((rows, sk), f32),
            pltpu.VMEM((rows, sk), f32),
            pltpu.VMEM((rows, whole), f32),
            pltpu.VMEM((nc, rows, CH), f32),
            pltpu.VMEM((nc, sk, CH), bf16),
            pltpu.VMEM((2 * rows + 16, CH), bf16),
            pltpu.VMEM((2 * rows + 16, sk), f32),
            pltpu.VMEM((rows, sk), bf16),
            pltpu.VMEM((rows, sk), bf16),
            pltpu.VMEM((rows, sk), bf16),
            dma((nc,)), dma((5,)), dma((nc,)), dma((nc,)), dma((nc,)), dma((nc,)), dma((2,)), dma((4,)), dma((4,)),
        ],
        compiler_params=pltpu.CompilerParams(
            collective_id=0, has_side_effects=True, vmem_limit_bytes=60 * 2**20
        ),
        cost_estimate=pl.CostEstimate(
            flops=2 * rows * ff * (2 * whole + 3 * sk), bytes_accessed=2 * (toks + 2 * rows) * ff, transcendentals=0
        ),
        name="gather_step_sketch",
    )(hidden, residual[0], cotangent[0], weight[0], self_sketch[0], mix_sketch[0], bucket[None], sign_bit[None])
    return tuple(o[None] for o in outs)


def solution(mesh):
    split = P("blk", "fsdp", None)
    return jax.shard_map(
        body,
        mesh=mesh,
        in_specs=(P(("blk", "fsdp"), None), split, split, split, split, split, P(), P()),
        out_specs=(split, split, split, split),
        check_vma=False,
    )
```

```python
import jax
import jax.numpy as jnp
from jax import lax
from jax.experimental import pallas as pl
from jax.experimental.pallas import tpu as pltpu
from jax.sharding import PartitionSpec as P

MESH = pl.DeviceIdType.MESH
STEP_SIZE = 0.3
CONSENSUS = 0.5
CH = 256
LANES = 128
LEAD = 4
GAP = 3
PARTS = 3


def nt(a, b):
    return lax.dot_general(a, b, (((1,), (1,)), ((), ())), preferred_element_type=jnp.float32)


def nn(a, b):
    return jnp.dot(a, b, preferred_element_type=jnp.float32)


def chunk_row(ref, j):
    parts = CH // LANES
    return jnp.concatenate([ref[pl.ds(j * parts + p, 1), :] for p in range(parts)], axis=1)


def signed_table(bkt, sgn, j, sk):
    sign = (2 * chunk_row(sgn, j) - 1).astype(jnp.float32)
    hot = lax.broadcasted_iota(jnp.int32, (sk, CH), 0) == chunk_row(bkt, j)
    return sign, jnp.where(hot, jnp.broadcast_to(sign, (sk, CH)), 0.0).astype(jnp.bfloat16)


def gather_kernel(
    hid, res, cot, wgt, slf, bkt, sgn,
    out_s, out_st, out_sk, out_left, out_right,
    buf, wv, cv, rv, sv, sacc, stepped, lhs, kacc, skf, sk_send,
    lsem, insem, sem1, sem2, sem3, sibsem, ssem, xsem, osem,
):
    rows, ff = wgt.shape
    toks = hid.shape[0]
    nc = ff // CH
    nb, nf = lax.axis_size("blk"), lax.axis_size("fsdp")
    sk = slf.shape[1]
    blk, me = lax.axis_index("blk"), lax.axis_index("fsdp")
    xh, y, core = me // 8, (me // 2) % 4, me % 2
    xo = 1 - xh

    def at(a, b):
        return a * 8 + (b % 4) * 2 + core

    sibling = me + 1 - 2 * core
    up, down, across = at(xh, y + 1), at(xh, y + 3), at(xo, y)
    ahead, behind = (blk + 1) % nb, (blk + nb - 1) % nb

    def block(j, b):
        return buf.at[j, pl.ds(pl.multiple_of(b * toks, toks), toks), :]

    def columns(ref, j):
        return ref.at[:, pl.ds(pl.multiple_of(j * CH, CH), CH)]

    def load(j):
        return pltpu.make_async_copy(columns(hid, j), block(j, me), lsem.at[j])

    def send(j, b, to, recv, lane):
        pltpu.make_async_remote_copy(
            src_ref=block(j, b), dst_ref=block(j, b), send_sem=ssem.at[lane], recv_sem=recv.at[j],
            device_id=(blk, to), device_id_type=MESH,
        ).start()

    def arrived(j, sem, blocks):
        ref = buf.at[j, pl.ds(0, blocks * toks), :]
        pltpu.make_async_copy(ref, ref, sem.at[j]).wait()

    def own(j):
        load(j).wait()
        send(j, me, up, sem1, 0)
        send(j, me, down, sem1, 0)
        send(j, me, across, sem1, 0)
        send(j, me, sibling, sibsem, 1)

    def second(j):
        arrived(j, sem1, 3)
        kind = (j % 3) // 2
        turn = 1 + 2 * (j % 2)
        send(j, at(xh, y + 4 - turn), at(xh, y + turn), sem2, 0)
        send(j, (1 - kind) * across + kind * up, (1 - kind) * up + kind * across, sem2, 0)
        send(j, (1 - kind) * across + kind * down, (1 - kind) * down + kind * across, sem2, 0)
        send(j, up, sibling, sibsem, 1)
        send(j, down, sibling, sibsem, 1)
        send(j, across, sibling, sibsem, 1)

    def third(j):
        arrived(j, sem2, 3)
        kind = (j % 3) // 2
        turn = 1 + 2 * (1 - j % 2)
        send(
            j,
            (1 - kind) * at(xh, y + 2) + kind * at(xo, y + 4 - turn),
            (1 - kind) * across + kind * at(xh, y + turn),
            sem3,
            0,
        )
        send(j, at(xh, y + 2), sibling, sibsem, 1)
        send(j, at(xo, y + 1), sibling, sibsem, 1)
        send(j, at(xo, y + 3), sibling, sibsem, 1)

    def fourth(j):
        arrived(j, sem3, 1)
        send(j, at(xo, y + 2), sibling, sibsem, 1)

    def put_stepped(j):
        return pltpu.make_async_copy(stepped.at[j], out_st.at[j], osem.at[0])

    def gradient_part(j):
        arrived(j, sibsem, nf // 2)
        w = wv[:, pl.ds(pl.multiple_of(j * CH, CH), CH)]
        new = w.astype(jnp.float32) - (STEP_SIZE * ff**-0.5) * nn(cv[...], buf[j])
        stepped[j] = new
        put_stepped(j).start()
        sign, table = signed_table(bkt, sgn, j, sk)
        high = new.astype(jnp.bfloat16)
        lhs[pl.ds(0, rows), :] = high
        lhs[pl.ds(rows, rows), :] = (new - high.astype(jnp.float32)).astype(jnp.bfloat16)
        lhs[pl.ds(2 * rows, 16), :] = jnp.broadcast_to(sign, (16, CH)).astype(jnp.bfloat16)
        kacc[...] += nt(lhs[...], table)

    def product_part(j):
        sacc[...] += nt(wv[:, pl.ds(pl.multiple_of(j * CH, CH), CH)], buf[j])

    barrier = pltpu.get_barrier_semaphore()
    for to in (up, down, across, sibling):
        pl.semaphore_signal(barrier, inc=1, device_id=(blk, to), device_id_type=MESH)
    for to in (ahead, behind):
        pl.semaphore_signal(barrier, inc=1, device_id=(to, me), device_id_type=MESH)

    def start_load(j, c):
        load(j).start()
        return c

    lax.fori_loop(0, LEAD, start_load, 0)
    pl.semaphore_wait(barrier, 6)

    def lead(j, c):
        own(j)
        return c

    lax.fori_loop(0, LEAD, lead, 0)
    lax.fori_loop(LEAD, nc, start_load, 0)
    ins = [(cot, cv), (wgt, wv), (res, rv), (slf, sv)]
    ins = [pltpu.make_async_copy(a, b, insem.at[i]) for i, (a, b) in enumerate(ins)]
    for c in ins:
        c.start()
    sacc[...] = jnp.zeros_like(sacc)
    kacc[...] = jnp.zeros_like(kacc)
    for c in ins:
        c.wait()

    last = 2 * GAP + 1

    def step(i, c):
        @pl.when(i + LEAD < nc)
        def _():
            own(i + LEAD)

        @pl.when(i >= last)
        def _():
            gradient_part(i - last)

        @pl.when(i < nc)
        def _():
            second(i)

        @pl.when((i >= GAP) & (i < nc + GAP))
        def _():
            third(i - GAP)

        @pl.when((i >= 2 * GAP) & (i < nc + 2 * GAP))
        def _():
            fourth(i - 2 * GAP)

        @pl.when((i >= last) & (i < nc + last - 1))
        def _():
            product_part(i - last)

        return c

    lax.fori_loop(0, nc + last, step, 0)

    sketched = (sk / ff) * (
        kacc[pl.ds(0, rows), :] + kacc[pl.ds(rows, rows), :] - kacc[pl.ds(2 * rows, 1), :] * sv[...]
    )
    sk_send[...] = sketched.astype(jnp.bfloat16)
    swaps = [
        pltpu.make_async_remote_copy(
            src_ref=sk_send, dst_ref=dst, send_sem=xsem.at[2 * i], recv_sem=xsem.at[2 * i + 1],
            device_id=(to, me), device_id_type=MESH,
        )
        for i, (dst, to) in enumerate(((out_left, ahead), (out_right, behind)))
    ]
    for c in swaps:
        c.start()
    skf[...] = sketched
    outs = [pltpu.make_async_copy(skf, out_sk, osem.at[1])]
    outs[0].start()
    product_part(nc - 1)
    rv[...] = (rv[...].astype(jnp.float32) + (ff**-0.5) * sacc[...]).astype(jnp.bfloat16)
    outs.append(pltpu.make_async_copy(rv, out_s, osem.at[2]))
    outs[1].start()
    outs.append(pltpu.make_async_copy(stepped, out_st, osem.at[0]))
    for lane, blocks in ((0, 7), (1, 8)):
        ref = buf.at[:, pl.ds(0, blocks * toks), :]
        pltpu.make_async_copy(ref, ref, ssem.at[lane]).wait()
    for c in outs + swaps:
        c.wait()


def update_kernel(
    st, sketch, left, right, slf, mix, bkt, sgn, stream,
    out_s, out_w, out_self, out_mix,
    stv, wv, av, lv, rv, sv, mv, dv, tv, insem, stsem, osem,
):
    nc = st.shape[0]
    sk = slf.shape[1]
    part = nc // PARTS

    def columns(ref, p):
        return ref.at[:, pl.ds(pl.multiple_of(p * part * CH, CH), part * CH)]

    def get(p):
        there = pl.ds(p * part, part)
        return pltpu.make_async_copy(st.at[there], stv.at[there], stsem.at[p])

    ins = [(left, lv), (right, rv), (sketch, av), (mix, mv), (slf, sv), (stream, tv)]
    ins = [pltpu.make_async_copy(a, b, insem.at[i]) for i, (a, b) in enumerate(ins)]
    for c in ins:
        c.start()
    for p in range(PARTS):
        get(p).start()
    for c in ins[:5]:
        c.wait()
    new_self = sv[...] + av[...]
    new_mix = mv[...] + (lv[...].astype(jnp.float32) + av[...] + rv[...].astype(jnp.float32)) / 3.0
    dv[...] = (CONSENSUS * (new_mix - new_self)).astype(jnp.bfloat16)
    sv[...] = new_self
    mv[...] = new_mix
    ins[5].wait()
    outs = [(sv, out_self), (mv, out_mix), (tv, out_s)]
    outs = [pltpu.make_async_copy(a, b, osem.at[i]) for i, (a, b) in enumerate(outs)]
    for c in outs:
        c.start()

    def expand(p, c):
        get(p).wait()
        for q in range(part):
            j = p * part + q
            _, table = signed_table(bkt, sgn, j, sk)
            new = stv[j] + nn(dv[...], table)
            wv[:, pl.ds(pl.multiple_of(j * CH, CH), CH)] = new.astype(jnp.bfloat16)
        pltpu.make_async_copy(columns(wv, p), columns(out_w, p), osem.at[3]).start()
        return c

    lax.fori_loop(0, PARTS, expand, 0)
    outs.append(pltpu.make_async_copy(wv, out_w, osem.at[3]))
    for c in outs:
        c.wait()


def body(hidden, residual, cotangent, weight, self_sketch, mix_sketch, bucket, sign_bit):
    toks, ff = hidden.shape
    _, rows, whole = residual.shape
    sk = self_sketch.shape[2]
    nc = ff // CH
    f32, bf16 = jnp.float32, jnp.bfloat16
    anywhere = pl.BlockSpec(memory_space=pl.ANY)
    vmem = pl.BlockSpec(memory_space=pltpu.VMEM)
    dma = pltpu.SemaphoreType.DMA
    shape = jax.ShapeDtypeStruct
    bkt, sgn = bucket.reshape(-1, LANES), sign_bit.reshape(-1, LANES)
    stream, stepped, sketched, left, right = pl.pallas_call(
        gather_kernel,
        out_shape=(
            shape((rows, whole), bf16),
            shape((nc, rows, CH), f32),
            shape((rows, sk), f32),
            shape((rows, sk), bf16),
            shape((rows, sk), bf16),
        ),
        in_specs=[anywhere] * 5 + [vmem] * 2,
        out_specs=(anywhere,) * 5,
        scratch_shapes=[
            pltpu.VMEM((nc, whole, CH), bf16),
            pltpu.VMEM((rows, ff), bf16),
            pltpu.VMEM((rows, whole), bf16),
            pltpu.VMEM((rows, whole), bf16),
            pltpu.VMEM((rows, sk), f32),
            pltpu.VMEM((rows, whole), f32),
            pltpu.VMEM((nc, rows, CH), f32),
            pltpu.VMEM((2 * rows + 16, CH), bf16),
            pltpu.VMEM((2 * rows + 16, sk), f32),
            pltpu.VMEM((rows, sk), f32),
            pltpu.VMEM((rows, sk), bf16),
            dma((nc,)), dma((4,)), dma((nc,)), dma((nc,)), dma((nc,)), dma((nc,)), dma((2,)), dma((4,)), dma((3,)),
        ],
        compiler_params=pltpu.CompilerParams(
            collective_id=0, has_side_effects=True, vmem_limit_bytes=58 * 2**20
        ),
        cost_estimate=pl.CostEstimate(
            flops=2 * rows * ff * (2 * whole + 2 * sk), bytes_accessed=2 * (toks + 2 * rows) * ff, transcendentals=0
        ),
        name="gather_step_sketch",
    )(hidden, residual[0], cotangent[0], weight[0], self_sketch[0], bkt, sgn)
    outs = pl.pallas_call(
        update_kernel,
        out_shape=(
            shape((rows, whole), bf16),
            shape((rows, ff), bf16),
            shape((rows, sk), f32),
            shape((rows, sk), f32),
        ),
        in_specs=[anywhere] * 6 + [vmem] * 2 + [anywhere],
        out_specs=(anywhere,) * 4,
        scratch_shapes=[
            pltpu.VMEM((nc, rows, CH), f32),
            pltpu.VMEM((rows, ff), bf16),
            pltpu.VMEM((rows, sk), f32),
            pltpu.VMEM((rows, sk), bf16),
            pltpu.VMEM((rows, sk), bf16),
            pltpu.VMEM((rows, sk), f32),
            pltpu.VMEM((rows, sk), f32),
            pltpu.VMEM((rows, sk), bf16),
            pltpu.VMEM((rows, whole), bf16),
            dma((6,)), dma((PARTS,)), dma((4,)),
        ],
        compiler_params=pltpu.CompilerParams(vmem_limit_bytes=58 * 2**20),
        cost_estimate=pl.CostEstimate(
            flops=2 * rows * ff * sk, bytes_accessed=6 * rows * ff, transcendentals=0
        ),
        name="update",
    )(stepped, sketched, left, right, self_sketch[0], mix_sketch[0], bkt, sgn, stream)
    return tuple(o[None] for o in outs)


def solution(mesh):
    split = P("blk", "fsdp", None)
    return jax.shard_map(
        body,
        mesh=mesh,
        in_specs=(P(("blk", "fsdp"), None), split, split, split, split, split, P(), P()),
        out_specs=(split, split, split, split),
        check_vma=False,
    )
```

```python
import jax
import jax.numpy as jnp
from jax import lax
from jax.experimental import pallas as pl
from jax.experimental.pallas import tpu as pltpu
from jax.sharding import PartitionSpec as P

MESH = pl.DeviceIdType.MESH
STEP_SIZE = 0.3
CONSENSUS = 0.5
CH = 256
LANES = 128
LEAD = 4
GAP = 2
PAIRS = 8
DEFER = 5
AHEAD = 4
FIRST_W = 2
OTHER = 2
LAG = 8
PIECES = 5
PARTS = 3


def nt(a, b):
    return lax.dot_general(a, b, (((1,), (1,)), ((), ())), preferred_element_type=jnp.float32)


def nn(a, b):
    return jnp.dot(a, b, preferred_element_type=jnp.float32)


def chunk_row(ref, j):
    parts = CH // LANES
    return jnp.concatenate([ref[pl.ds(j * parts + p, 1), :] for p in range(parts)], axis=1)


def signed_table(bkt, sgn, j, sk):
    sign = (2 * chunk_row(sgn, j) - 1).astype(jnp.float32)
    hot = lax.broadcasted_iota(jnp.int32, (sk, CH), 0) == chunk_row(bkt, j)
    return sign, jnp.where(hot, jnp.broadcast_to(sign, (sk, CH)), 0.0).astype(jnp.bfloat16)


def gather_kernel(
    hid, res, cot, wgt, slf, bkt, sgn,
    out_s, out_st, out_sk, out_left, out_right,
    buf, wv, cv, rv, sv, sacc, stepped, lhs, kacc, skf, sk_send, wpart, gsend, grecv, psend, precv,
    lsem, insem, sem1, sem2, sem3, sibsem, ssem, xsem, osem, gsem, wsem, psem,
):
    rows, ff = wgt.shape
    toks = hid.shape[0]
    nc = ff // CH
    slots = nc - PAIRS
    nb, nf = lax.axis_size("blk"), lax.axis_size("fsdp")
    sk = slf.shape[1]
    blk, me = lax.axis_index("blk"), lax.axis_index("fsdp")
    xh, y, core = me // 8, (me // 2) % 4, me % 2
    xo = 1 - xh

    def at(a, b):
        return a * 8 + (b % 4) * 2 + core

    sibling = me + 1 - 2 * core
    up, down, across = at(xh, y + 1), at(xh, y + 3), at(xo, y)
    ahead, behind = (blk + 1) % nb, (blk + nb - 1) % nb

    def chunk(i, half):
        paired = (slots + PAIRS - 1 - i) // slots
        return paired * (2 * i + half) + (1 - paired) * (i + PAIRS)

    def block(j, b):
        return buf.at[j, pl.ds(pl.multiple_of(b * toks, toks), toks), :]

    def span(j):
        return pl.ds(pl.multiple_of(j * CH, CH), CH)

    def load(j):
        return pltpu.make_async_copy(hid.at[:, span(j)], block(j, me), lsem.at[j])

    def send(i, j, b, to, recv, lane):
        pltpu.make_async_remote_copy(
            src_ref=block(j, b), dst_ref=block(j, b), send_sem=ssem.at[lane], recv_sem=recv.at[i],
            device_id=(blk, to), device_id_type=MESH,
        ).start()

    def hand(src, dst, recv, lane):
        pltpu.make_async_remote_copy(
            src_ref=src, dst_ref=dst, send_sem=ssem.at[lane], recv_sem=recv,
            device_id=(blk, across), device_id_type=MESH,
        ).start()

    def landed(ref, sem):
        pltpu.make_async_copy(ref, ref, sem).wait()

    def arrived(i, sem, blocks):
        landed(buf.at[i, pl.ds(0, blocks * toks), :], sem.at[i])

    def cross(i):
        other = chunk(i, xo)
        load(other).wait()
        send(i, other, me, across, sem1, 0)

    def own(i):
        j = chunk(i, xh)

        @pl.when(i < PAIRS)
        def _():
            load(j).wait()

        send(i, j, me, up, sem1, 0)
        send(i, j, me, down, sem1, 0)
        send(i, j, me, sibling, sibsem, 1)

    def second(i):
        arrived(i, sem1, 3)
        j = chunk(i, xh)
        turn = 1 + 2 * (i % 2)
        send(i, j, at(xh, y + 4 - turn), at(xh, y + turn), sem2, 0)
        send(i, j, across, up, sem2, 0)
        send(i, j, across, down, sem2, 0)
        send(i, j, up, sibling, sibsem, 1)
        send(i, j, down, sibling, sibsem, 1)
        send(i, j, across, sibling, sibsem, 1)

    def third(i):
        arrived(i, sem2, 3)
        j = chunk(i, xh)
        turn = 1 + 2 * (1 - i % 2)
        send(i, j, at(xo, y + 4 - turn), at(xh, y + turn), sem3, 0)
        send(i, j, at(xh, y + 2), sibling, sibsem, 1)
        send(i, j, at(xo, y + 1), sibling, sibsem, 1)
        send(i, j, at(xo, y + 3), sibling, sibsem, 1)

    def fourth(i):
        arrived(i, sem3, 1)
        send(i, chunk(i, xh), at(xo, y + 2), sibling, sibsem, 1)

    def finish(j, gradient):
        new = wv[:, span(j)].astype(jnp.float32) - (STEP_SIZE * ff**-0.5) * gradient
        stepped[j] = new
        pltpu.make_async_copy(stepped.at[j], out_st.at[j], osem.at[0]).start()
        sign, table = signed_table(bkt, sgn, j, sk)
        high = new.astype(jnp.bfloat16)
        lhs[pl.ds(0, rows), :] = high
        lhs[pl.ds(rows, rows), :] = (new - high.astype(jnp.float32)).astype(jnp.bfloat16)
        lhs[pl.ds(2 * rows, 16), :] = jnp.broadcast_to(sign, (16, CH)).astype(jnp.bfloat16)
        kacc[...] += nt(lhs[...], table)

    mine, theirs = pl.ds(0, rows), pl.ds(rows, rows)

    def paired_step(k):
        arrived(k, sibsem, nf // 2)
        landed(wpart.at[k], wsem.at[k])
        j = chunk(k, xh)
        h = buf[j]
        both = nn(cv[...], h)
        gsend[k] = both[rows:].astype(jnp.bfloat16)
        hand(gsend.at[k], grecv.at[k], gsem.at[k], 4)
        finish(j, both[:rows])
        sacc[...] += nt(jnp.concatenate([wv[:, span(j)], wpart[k]], axis=0), h)

    def other_step(k):
        landed(grecv.at[k], gsem.at[k])
        finish(chunk(k, xo), grecv[k].astype(jnp.float32))

    def gradient_part(i):
        arrived(i, sibsem, nf // 2)
        j = chunk(i, xh)
        finish(j, nn(cv[mine, :], buf[j]))

    def product_part(i):
        j = chunk(i, xh)
        sacc[mine, :] += nt(wv[:, span(j)], buf[j])

    barrier = pltpu.get_barrier_semaphore()
    for to in (up, down, across, sibling):
        pl.semaphore_signal(barrier, inc=1, device_id=(blk, to), device_id_type=MESH)
    for to in (ahead, behind):
        pl.semaphore_signal(barrier, inc=1, device_id=(to, me), device_id_type=MESH)

    def start_load(j, c):
        load(j).start()
        return c

    lax.fori_loop(0, 2 * AHEAD, start_load, 0)
    ins = [(cot, cv.at[mine, :]), (wgt, wv), (res, rv), (slf, sv)]
    ins = [pltpu.make_async_copy(a, b, insem.at[i]) for i, (a, b) in enumerate(ins)]
    ins[0].start()
    pl.semaphore_wait(barrier, 6)

    def lead(i, c):
        cross(i)
        own(i)
        return c

    def lead_cross(i, c):
        cross(i)
        return c

    lax.fori_loop(0, LEAD, lead, 0)
    for c in ins[1:]:
        c.start()
    lax.fori_loop(2 * AHEAD, nc, start_load, 0)
    lax.fori_loop(LEAD, AHEAD, lead_cross, 0)
    sacc[...] = jnp.zeros_like(sacc)
    kacc[...] = jnp.zeros_like(kacc)
    for c in ins:
        c.wait()

    last = 2 * GAP + 1
    strip = rows // PIECES
    first_sum = LAG + PAIRS

    def step(i, c):
        @pl.when(i + AHEAD < slots)
        def _():
            cross(i + AHEAD)

        @pl.when(i + LEAD < slots)
        def _():
            own(i + LEAD)

        @pl.when(i == 0)
        def _():
            for p in range(PIECES):
                hand(cv.at[pl.ds(p * strip, strip), :], cv.at[pl.ds(rows + p * strip, strip), :], psem.at[0], 2)

        @pl.when((i >= FIRST_W) & (i < FIRST_W + PAIRS // 2))
        def _():
            for q in range(2):
                k = 2 * (i - FIRST_W) + q
                hand(wv.at[:, span(chunk(k, xo))], wpart.at[k], wsem.at[k], 3)

        @pl.when((i >= first_sum) & (i < first_sum + PIECES))
        def _():
            at_row = pl.multiple_of((i - first_sum) * strip, strip)
            there = pl.ds(at_row, strip)
            psend[there, :] = sacc[pl.ds(rows + at_row, strip), :].astype(jnp.bfloat16)
            hand(psend.at[there, :], precv.at[there, :], psem.at[1], 5)

        @pl.when(i < slots)
        def _():
            second(i)

        @pl.when((i >= GAP) & (i < slots + GAP))
        def _():
            third(i - GAP)

        @pl.when((i >= 2 * GAP) & (i < slots + 2 * GAP))
        def _():
            fourth(i - 2 * GAP)

        @pl.when(i >= PAIRS + last)
        def _():
            gradient_part(i - last)

        @pl.when(i == LAG)
        def _():
            landed(cv.at[theirs, :], psem.at[0])

        @pl.when((i >= LAG) & (i < first_sum))
        def _():
            paired_step(i - LAG)

        @pl.when((i >= (LAG + OTHER)) & (i < (LAG + OTHER) + PAIRS))
        def _():
            other_step(i - (LAG + OTHER))

        @pl.when(i >= PAIRS + last + DEFER)
        def _():
            product_part(i - last - DEFER)

        return c

    lax.fori_loop(0, slots + last, step, 0)

    sketched = (sk / ff) * (
        kacc[pl.ds(0, rows), :] + kacc[pl.ds(rows, rows), :] - kacc[pl.ds(2 * rows, 1), :] * sv[...]
    )
    sk_send[...] = sketched.astype(jnp.bfloat16)
    swaps = [
        pltpu.make_async_remote_copy(
            src_ref=sk_send, dst_ref=dst, send_sem=xsem.at[2 * i], recv_sem=xsem.at[2 * i + 1],
            device_id=(to, me), device_id_type=MESH,
        )
        for i, (dst, to) in enumerate(((out_left, ahead), (out_right, behind)))
    ]
    for c in swaps:
        c.start()
    skf[...] = sketched
    outs = [pltpu.make_async_copy(skf, out_sk, osem.at[1])]
    outs[0].start()

    def product_left(i, c):
        product_part(i)
        return c

    lax.fori_loop(slots - DEFER, slots, product_left, 0)
    landed(precv, psem.at[1])
    total = sacc[mine, :] + precv[...].astype(jnp.float32)
    rv[...] = (rv[...].astype(jnp.float32) + (ff**-0.5) * total).astype(jnp.bfloat16)
    outs.append(pltpu.make_async_copy(rv, out_s, osem.at[2]))
    outs[1].start()
    outs.append(pltpu.make_async_copy(stepped, out_st, osem.at[0]))
    for lane, blocks in ((0, 7), (1, 8)):
        landed(buf.at[pl.ds(0, slots), pl.ds(0, blocks * toks), :], ssem.at[lane])
    for i, ref in enumerate((cv.at[theirs, :], wpart, gsend, precv)):
        landed(ref, ssem.at[2 + i])
    for c in outs + swaps:
        c.wait()


def update_kernel(
    st, sketch, left, right, slf, mix, bkt, sgn, stream,
    out_s, out_w, out_self, out_mix,
    stv, wv, av, lv, rv, sv, mv, dv, tv, insem, stsem, osem,
):
    nc = st.shape[0]
    sk = slf.shape[1]
    part = nc // PARTS

    def columns(ref, p):
        return ref.at[:, pl.ds(pl.multiple_of(p * part * CH, CH), part * CH)]

    def get(p):
        there = pl.ds(p * part, part)
        return pltpu.make_async_copy(st.at[there], stv.at[there], stsem.at[p])

    ins = [(left, lv), (right, rv), (sketch, av), (mix, mv), (slf, sv), (stream, tv)]
    ins = [pltpu.make_async_copy(a, b, insem.at[i]) for i, (a, b) in enumerate(ins)]
    for c in ins:
        c.start()
    for p in range(PARTS):
        get(p).start()
    for c in ins[:5]:
        c.wait()
    new_self = sv[...] + av[...]
    new_mix = mv[...] + (lv[...].astype(jnp.float32) + av[...] + rv[...].astype(jnp.float32)) / 3.0
    dv[...] = (CONSENSUS * (new_mix - new_self)).astype(jnp.bfloat16)
    sv[...] = new_self
    mv[...] = new_mix
    ins[5].wait()
    outs = [(sv, out_self), (mv, out_mix), (tv, out_s)]
    outs = [pltpu.make_async_copy(a, b, osem.at[i]) for i, (a, b) in enumerate(outs)]
    for c in outs:
        c.start()

    def expand(p, c):
        get(p).wait()
        for q in range(part):
            j = p * part + q
            _, table = signed_table(bkt, sgn, j, sk)
            new = stv[j] + nn(dv[...], table)
            wv[:, pl.ds(pl.multiple_of(j * CH, CH), CH)] = new.astype(jnp.bfloat16)
        pltpu.make_async_copy(columns(wv, p), columns(out_w, p), osem.at[3]).start()
        return c

    lax.fori_loop(0, PARTS, expand, 0)
    outs.append(pltpu.make_async_copy(wv, out_w, osem.at[3]))
    for c in outs:
        c.wait()


def body(hidden, residual, cotangent, weight, self_sketch, mix_sketch, bucket, sign_bit):
    toks, ff = hidden.shape
    _, rows, whole = residual.shape
    sk = self_sketch.shape[2]
    nc = ff // CH
    f32, bf16 = jnp.float32, jnp.bfloat16
    anywhere = pl.BlockSpec(memory_space=pl.ANY)
    vmem = pl.BlockSpec(memory_space=pltpu.VMEM)
    dma = pltpu.SemaphoreType.DMA
    shape = jax.ShapeDtypeStruct
    bkt, sgn = bucket.reshape(-1, LANES), sign_bit.reshape(-1, LANES)
    stream, stepped, sketched, left, right = pl.pallas_call(
        gather_kernel,
        out_shape=(
            shape((rows, whole), bf16),
            shape((nc, rows, CH), f32),
            shape((rows, sk), f32),
            shape((rows, sk), bf16),
            shape((rows, sk), bf16),
        ),
        in_specs=[anywhere] * 5 + [vmem] * 2,
        out_specs=(anywhere,) * 5,
        scratch_shapes=[
            pltpu.VMEM((nc, whole, CH), bf16),
            pltpu.VMEM((rows, ff), bf16),
            pltpu.VMEM((2 * rows, whole), bf16),
            pltpu.VMEM((rows, whole), bf16),
            pltpu.VMEM((rows, sk), f32),
            pltpu.VMEM((2 * rows, whole), f32),
            pltpu.VMEM((nc, rows, CH), f32),
            pltpu.VMEM((2 * rows + 16, CH), bf16),
            pltpu.VMEM((2 * rows + 16, sk), f32),
            pltpu.VMEM((rows, sk), f32),
            pltpu.VMEM((rows, sk), bf16),
            pltpu.VMEM((PAIRS, rows, CH), bf16),
            pltpu.VMEM((PAIRS, rows, CH), bf16),
            pltpu.VMEM((PAIRS, rows, CH), bf16),
            pltpu.VMEM((rows, whole), bf16),
            pltpu.VMEM((rows, whole), bf16),
            dma((nc,)), dma((4,)), dma((nc,)), dma((nc,)), dma((nc,)), dma((nc,)), dma((6,)), dma((4,)), dma((3,)),
            dma((PAIRS,)), dma((PAIRS,)), dma((2,)),
        ],
        compiler_params=pltpu.CompilerParams(
            collective_id=0, has_side_effects=True, vmem_limit_bytes=58 * 2**20
        ),
        cost_estimate=pl.CostEstimate(
            flops=2 * rows * ff * (2 * whole + 2 * sk), bytes_accessed=2 * (toks + 2 * rows) * ff, transcendentals=0
        ),
        name="gather_step_sketch",
    )(hidden, residual[0], cotangent[0], weight[0], self_sketch[0], bkt, sgn)
    outs = pl.pallas_call(
        update_kernel,
        out_shape=(
            shape((rows, whole), bf16),
            shape((rows, ff), bf16),
            shape((rows, sk), f32),
            shape((rows, sk), f32),
        ),
        in_specs=[anywhere] * 6 + [vmem] * 2 + [anywhere],
        out_specs=(anywhere,) * 4,
        scratch_shapes=[
            pltpu.VMEM((nc, rows, CH), f32),
            pltpu.VMEM((rows, ff), bf16),
            pltpu.VMEM((rows, sk), f32),
            pltpu.VMEM((rows, sk), bf16),
            pltpu.VMEM((rows, sk), bf16),
            pltpu.VMEM((rows, sk), f32),
            pltpu.VMEM((rows, sk), f32),
            pltpu.VMEM((rows, sk), bf16),
            pltpu.VMEM((rows, whole), bf16),
            dma((6,)), dma((PARTS,)), dma((4,)),
        ],
        compiler_params=pltpu.CompilerParams(vmem_limit_bytes=58 * 2**20),
        cost_estimate=pl.CostEstimate(
            flops=2 * rows * ff * sk, bytes_accessed=6 * rows * ff, transcendentals=0
        ),
        name="update",
    )(stepped, sketched, left, right, self_sketch[0], mix_sketch[0], bkt, sgn, stream)
    return tuple(o[None] for o in outs)


def solution(mesh):
    split = P("blk", "fsdp", None)
    return jax.shard_map(
        body,
        mesh=mesh,
        in_specs=(P(("blk", "fsdp"), None), split, split, split, split, split, P(), P()),
        out_specs=(split, split, split, split),
        check_vma=False,
    )
```

```python
import jax
import jax.numpy as jnp
from jax import lax
from jax.experimental import pallas as pl
from jax.experimental.pallas import tpu as pltpu
from jax.sharding import PartitionSpec as P

MESH = pl.DeviceIdType.MESH
STEP_SIZE = 0.3
CONSENSUS = 0.5
CH = 256
LANES = 128
LEAD = 4
GAP = 2
PAIRS = 8
DEFER = 5
AHEAD = 4
FIRST_W = 2
OTHER = 2
LAG = 8
PIECES = 5
PARTS = 3
PUT = 3


def nt(a, b):
    return lax.dot_general(a, b, (((1,), (1,)), ((), ())), preferred_element_type=jnp.float32)


def nn(a, b):
    return jnp.dot(a, b, preferred_element_type=jnp.float32)


def chunk_row(ref, j):
    parts = CH // LANES
    return jnp.concatenate([ref[pl.ds(j * parts + p, 1), :] for p in range(parts)], axis=1)


def signed_table(bkt, sgn, j, sk):
    sign = (2 * chunk_row(sgn, j) - 1).astype(jnp.float32)
    hot = lax.broadcasted_iota(jnp.int32, (sk, CH), 0) == chunk_row(bkt, j)
    return sign, jnp.where(hot, jnp.broadcast_to(sign, (sk, CH)), 0.0).astype(jnp.bfloat16)


def gather_kernel(
    hid, res, cot, wgt, slf, bucket, bits,
    out_s, out_st, out_sk, out_left, out_right,
    buf, wv, cv, rv, sv, sacc, stepped, lhs, kacc, skf, sk_send, wpart, gsend, grecv, psend, precv, bkt, sgn,
    lsem, insem, sem1, sem2, sem3, sibsem, ssem, xsem, osem, gsem, wsem, psem,
):
    rows, ff = wgt.shape
    toks = hid.shape[0]
    nc = ff // CH
    slots = nc - PAIRS
    nb, nf = lax.axis_size("blk"), lax.axis_size("fsdp")
    sk = slf.shape[1]
    blk, me = lax.axis_index("blk"), lax.axis_index("fsdp")
    xh, y, core = me // 8, (me // 2) % 4, me % 2
    xo = 1 - xh

    def at(a, b):
        return a * 8 + (b % 4) * 2 + core

    sibling = me + 1 - 2 * core
    up, down, across = at(xh, y + 1), at(xh, y + 3), at(xo, y)
    ahead, behind = (blk + 1) % nb, (blk + nb - 1) % nb

    def chunk(i, half):
        paired = (slots + PAIRS - 1 - i) // slots
        return paired * (2 * i + half) + (1 - paired) * (i + PAIRS)

    def block(j, b):
        return buf.at[j, pl.ds(pl.multiple_of(b * toks, toks), toks), :]

    def span(j):
        return pl.ds(pl.multiple_of(j * CH, CH), CH)

    def load(j):
        return pltpu.make_async_copy(hid.at[:, span(j)], block(j, me), lsem.at[j])

    def send(i, j, b, to, recv, lane):
        pltpu.make_async_remote_copy(
            src_ref=block(j, b), dst_ref=block(j, b), send_sem=ssem.at[lane], recv_sem=recv.at[i],
            device_id=(blk, to), device_id_type=MESH,
        ).start()

    def hand(src, dst, recv, lane):
        pltpu.make_async_remote_copy(
            src_ref=src, dst_ref=dst, send_sem=ssem.at[lane], recv_sem=recv,
            device_id=(blk, across), device_id_type=MESH,
        ).start()

    def landed(ref, sem):
        pltpu.make_async_copy(ref, ref, sem).wait()

    def arrived(i, sem, blocks):
        landed(buf.at[i, pl.ds(0, blocks * toks), :], sem.at[i])

    def cross(i):
        other = chunk(i, xo)
        load(other).wait()
        send(i, other, me, across, sem1, 0)

    def own(i):
        j = chunk(i, xh)

        @pl.when(i < PAIRS)
        def _():
            load(j).wait()

        send(i, j, me, up, sem1, 0)
        send(i, j, me, down, sem1, 0)
        send(i, j, me, sibling, sibsem, 1)

    def second(i):
        arrived(i, sem1, 3)
        j = chunk(i, xh)
        turn = 1 + 2 * (i % 2)
        send(i, j, at(xh, y + 4 - turn), at(xh, y + turn), sem2, 0)
        send(i, j, across, up, sem2, 0)
        send(i, j, across, down, sem2, 0)
        send(i, j, up, sibling, sibsem, 1)
        send(i, j, down, sibling, sibsem, 1)
        send(i, j, across, sibling, sibsem, 1)

    def third(i):
        arrived(i, sem2, 3)
        j = chunk(i, xh)
        turn = 1 + 2 * (1 - i % 2)
        send(i, j, at(xo, y + 4 - turn), at(xh, y + turn), sem3, 0)
        send(i, j, at(xh, y + 2), sibling, sibsem, 1)
        send(i, j, at(xo, y + 1), sibling, sibsem, 1)
        send(i, j, at(xo, y + 3), sibling, sibsem, 1)

    def fourth(i):
        arrived(i, sem3, 1)
        send(i, chunk(i, xh), at(xo, y + 2), sibling, sibsem, 1)

    def finish(j, gradient):
        new = wv[:, span(j)].astype(jnp.float32) - (STEP_SIZE * ff**-0.5) * gradient
        stepped[j] = new
        pltpu.make_async_copy(stepped.at[j], out_st.at[j], osem.at[0]).start()
        sign, table = signed_table(bkt, sgn, j, sk)
        high = new.astype(jnp.bfloat16)
        lhs[pl.ds(0, rows), :] = high
        lhs[pl.ds(rows, rows), :] = (new - high.astype(jnp.float32)).astype(jnp.bfloat16)
        lhs[pl.ds(2 * rows, 16), :] = jnp.broadcast_to(sign, (16, CH)).astype(jnp.bfloat16)
        kacc[...] += nt(lhs[...], table)

    mine, theirs = pl.ds(0, rows), pl.ds(rows, rows)

    def paired_step(k):
        arrived(k, sibsem, nf // 2)
        landed(wpart.at[k], wsem.at[k])
        j = chunk(k, xh)
        h = buf[j]
        both = nn(cv[...], h)
        gsend[k] = both[rows:].astype(jnp.bfloat16)
        hand(gsend.at[k], grecv.at[k], gsem.at[k], 4)
        finish(j, both[:rows])
        sacc[...] += nt(jnp.concatenate([wv[:, span(j)], wpart[k]], axis=0), h)

    def other_step(k):
        landed(grecv.at[k], gsem.at[k])
        finish(chunk(k, xo), grecv[k].astype(jnp.float32))

    def gradient_part(i):
        arrived(i, sibsem, nf // 2)
        j = chunk(i, xh)
        finish(j, nn(cv[mine, :], buf[j]))

    def product_part(i):
        j = chunk(i, xh)
        sacc[mine, :] += nt(wv[:, span(j)], buf[j])

    barrier = pltpu.get_barrier_semaphore()
    for to in (up, down, across, sibling):
        pl.semaphore_signal(barrier, inc=1, device_id=(blk, to), device_id_type=MESH)
    for to in (ahead, behind):
        pl.semaphore_signal(barrier, inc=1, device_id=(to, me), device_id_type=MESH)

    def start_load(j, c):
        load(j).start()
        return c

    lax.fori_loop(0, 2 * AHEAD, start_load, 0)
    ins = [(cot, cv.at[mine, :]), (wgt, wv), (bucket, bkt), (bits, sgn), (slf, sv), (res, rv)]
    ins = [pltpu.make_async_copy(a, b, insem.at[i]) for i, (a, b) in enumerate(ins)]
    ins[0].start()
    pl.semaphore_wait(barrier, 6)

    def lead(i, c):
        cross(i)
        own(i)
        return c

    def lead_cross(i, c):
        cross(i)
        return c

    lax.fori_loop(0, LEAD, lead, 0)
    for c in ins[1:]:
        c.start()
    lax.fori_loop(2 * AHEAD, nc, start_load, 0)
    lax.fori_loop(LEAD, AHEAD, lead_cross, 0)
    sacc[...] = jnp.zeros_like(sacc)
    kacc[...] = jnp.zeros_like(kacc)
    for c in ins:
        c.wait()

    last = 2 * GAP + 1
    strip = rows // PIECES
    first_sum = LAG + PAIRS

    def step(i, c):
        @pl.when(i + AHEAD < slots)
        def _():
            cross(i + AHEAD)

        @pl.when(i + LEAD < slots)
        def _():
            own(i + LEAD)

        @pl.when(i == 0)
        def _():
            for p in range(PIECES):
                hand(cv.at[pl.ds(p * strip, strip), :], cv.at[pl.ds(rows + p * strip, strip), :], psem.at[0], 2)

        @pl.when((i >= FIRST_W) & (i < FIRST_W + PAIRS // 2))
        def _():
            for q in range(2):
                k = 2 * (i - FIRST_W) + q
                hand(wv.at[:, span(chunk(k, xo))], wpart.at[k], wsem.at[k], 3)

        @pl.when(i == first_sum)
        def _():
            psend[...] = sacc[theirs, :].astype(jnp.bfloat16)
            for p in range(PIECES):
                there = pl.ds(p * strip, strip)
                hand(psend.at[there, :], precv.at[there, :], psem.at[1], 5)

        @pl.when(i < slots)
        def _():
            second(i)

        @pl.when((i >= GAP) & (i < slots + GAP))
        def _():
            third(i - GAP)

        @pl.when((i >= 2 * GAP) & (i < slots + 2 * GAP))
        def _():
            fourth(i - 2 * GAP)

        @pl.when(i >= PAIRS + last)
        def _():
            gradient_part(i - last)

        @pl.when(i == LAG)
        def _():
            landed(cv.at[theirs, :], psem.at[0])

        @pl.when((i >= LAG) & (i < first_sum))
        def _():
            paired_step(i - LAG)

        @pl.when((i >= (LAG + OTHER)) & (i < (LAG + OTHER) + PAIRS))
        def _():
            other_step(i - (LAG + OTHER))

        @pl.when(i >= PAIRS + last + DEFER)
        def _():
            product_part(i - last - DEFER)

        return c

    lax.fori_loop(0, slots + last, step, 0)

    sketched = (sk / ff) * (
        kacc[pl.ds(0, rows), :] + kacc[pl.ds(rows, rows), :] - kacc[pl.ds(2 * rows, 1), :] * sv[...]
    )
    sk_send[...] = sketched.astype(jnp.bfloat16)
    swaps = [
        pltpu.make_async_remote_copy(
            src_ref=sk_send, dst_ref=dst, send_sem=xsem.at[2 * i], recv_sem=xsem.at[2 * i + 1],
            device_id=(to, me), device_id_type=MESH,
        )
        for i, (dst, to) in enumerate(((out_left, ahead), (out_right, behind)))
    ]
    for c in swaps:
        c.start()
    skf[...] = sketched
    outs = [pltpu.make_async_copy(skf, out_sk, osem.at[1])]
    outs[0].start()

    def product_left(i, c):
        product_part(i)
        return c

    lax.fori_loop(slots - DEFER, slots, product_left, 0)
    landed(precv, psem.at[1])
    total = sacc[mine, :] + precv[...].astype(jnp.float32)
    rv[...] = (rv[...].astype(jnp.float32) + (ff**-0.5) * total).astype(jnp.bfloat16)
    outs.append(pltpu.make_async_copy(rv, out_s, osem.at[2]))
    outs[1].start()
    outs.append(pltpu.make_async_copy(stepped, out_st, osem.at[0]))
    for lane, blocks in ((0, 7), (1, 8)):
        landed(buf.at[pl.ds(0, slots), pl.ds(0, blocks * toks), :], ssem.at[lane])
    for i, ref in enumerate((cv.at[theirs, :], wpart, gsend, precv)):
        landed(ref, ssem.at[2 + i])
    for c in outs + swaps:
        c.wait()


def update_kernel(
    st, sketch, left, right, slf, mix, bucket, bits, stream,
    out_s, out_w, out_self, out_mix,
    stv, wv, av, lv, rv, sv, mv, dv, tv, bkt, sgn, insem, stsem, osem,
):
    nc = st.shape[0]
    sk = slf.shape[1]
    part = nc // PARTS

    def columns(ref, j):
        return ref.at[:, pl.ds(pl.multiple_of(j * CH, CH), PUT * CH)]

    def get(p):
        there = pl.ds(p * part, part)
        return pltpu.make_async_copy(st.at[there], stv.at[there], stsem.at[p])

    ins = [(left, lv), (right, rv), (sketch, av), (mix, mv), (slf, sv), (bucket, bkt), (bits, sgn), (stream, tv)]
    ins = [pltpu.make_async_copy(a, b, insem.at[i]) for i, (a, b) in enumerate(ins)]
    for c in ins:
        c.start()
    for p in range(PARTS):
        get(p).start()
    for c in ins[:7]:
        c.wait()
    new_self = sv[...] + av[...]
    new_mix = mv[...] + (lv[...].astype(jnp.float32) + av[...] + rv[...].astype(jnp.float32)) / 3.0
    dv[...] = (CONSENSUS * (new_mix - new_self)).astype(jnp.bfloat16)
    sv[...] = new_self
    mv[...] = new_mix
    ins[7].wait()
    outs = [(sv, out_self), (mv, out_mix), (tv, out_s)]
    outs = [pltpu.make_async_copy(a, b, osem.at[i]) for i, (a, b) in enumerate(outs)]
    for c in outs:
        c.start()

    def expand(p, c):
        get(p).wait()
        for q in range(part):
            j = p * part + q
            _, table = signed_table(bkt, sgn, j, sk)
            new = stv[j] + nn(dv[...], table)
            wv[:, pl.ds(pl.multiple_of(j * CH, CH), CH)] = new.astype(jnp.bfloat16)
            if q % PUT == PUT - 1:
                there = j - PUT + 1
                pltpu.make_async_copy(columns(wv, there), columns(out_w, there), osem.at[3]).start()
        return c

    lax.fori_loop(0, PARTS, expand, 0)
    outs.append(pltpu.make_async_copy(wv, out_w, osem.at[3]))
    for c in outs:
        c.wait()


def body(hidden, residual, cotangent, weight, self_sketch, mix_sketch, bucket, sign_bit):
    toks, ff = hidden.shape
    _, rows, whole = residual.shape
    sk = self_sketch.shape[2]
    nc = ff // CH
    f32, bf16 = jnp.float32, jnp.bfloat16
    anywhere = pl.BlockSpec(memory_space=pl.ANY)
    dma = pltpu.SemaphoreType.DMA
    shape = jax.ShapeDtypeStruct
    bkt, sgn = bucket.reshape(-1, LANES), sign_bit.reshape(-1, LANES)
    stream, stepped, sketched, left, right = pl.pallas_call(
        gather_kernel,
        out_shape=(
            shape((rows, whole), bf16),
            shape((nc, rows, CH), f32),
            shape((rows, sk), f32),
            shape((rows, sk), bf16),
            shape((rows, sk), bf16),
        ),
        in_specs=[anywhere] * 7,
        out_specs=(anywhere,) * 5,
        scratch_shapes=[
            pltpu.VMEM((nc, whole, CH), bf16),
            pltpu.VMEM((rows, ff), bf16),
            pltpu.VMEM((2 * rows, whole), bf16),
            pltpu.VMEM((rows, whole), bf16),
            pltpu.VMEM((rows, sk), f32),
            pltpu.VMEM((2 * rows, whole), f32),
            pltpu.VMEM((nc, rows, CH), f32),
            pltpu.VMEM((2 * rows + 16, CH), bf16),
            pltpu.VMEM((2 * rows + 16, sk), f32),
            pltpu.VMEM((rows, sk), f32),
            pltpu.VMEM((rows, sk), bf16),
            pltpu.VMEM((PAIRS, rows, CH), bf16),
            pltpu.VMEM((PAIRS, rows, CH), bf16),
            pltpu.VMEM((PAIRS, rows, CH), bf16),
            pltpu.VMEM((rows, whole), bf16),
            pltpu.VMEM((rows, whole), bf16),
            pltpu.VMEM(bkt.shape, jnp.int32),
            pltpu.VMEM(bkt.shape, jnp.int32),
            dma((nc,)), dma((6,)), dma((nc,)), dma((nc,)), dma((nc,)), dma((nc,)), dma((6,)), dma((4,)), dma((3,)),
            dma((PAIRS,)), dma((PAIRS,)), dma((2,)),
        ],
        compiler_params=pltpu.CompilerParams(
            collective_id=0, has_side_effects=True, vmem_limit_bytes=58 * 2**20
        ),
        cost_estimate=pl.CostEstimate(
            flops=2 * rows * ff * (2 * whole + 2 * sk), bytes_accessed=2 * (toks + 2 * rows) * ff, transcendentals=0
        ),
        name="gather_step_sketch",
    )(hidden, residual[0], cotangent[0], weight[0], self_sketch[0], bkt, sgn)
    outs = pl.pallas_call(
        update_kernel,
        out_shape=(
            shape((rows, whole), bf16),
            shape((rows, ff), bf16),
            shape((rows, sk), f32),
            shape((rows, sk), f32),
        ),
        in_specs=[anywhere] * 9,
        out_specs=(anywhere,) * 4,
        scratch_shapes=[
            pltpu.VMEM((nc, rows, CH), f32),
            pltpu.VMEM((rows, ff), bf16),
            pltpu.VMEM((rows, sk), f32),
            pltpu.VMEM((rows, sk), bf16),
            pltpu.VMEM((rows, sk), bf16),
            pltpu.VMEM((rows, sk), f32),
            pltpu.VMEM((rows, sk), f32),
            pltpu.VMEM((rows, sk), bf16),
            pltpu.VMEM((rows, whole), bf16),
            pltpu.VMEM(bkt.shape, jnp.int32),
            pltpu.VMEM(bkt.shape, jnp.int32),
            dma((8,)), dma((PARTS,)), dma((4,)),
        ],
        compiler_params=pltpu.CompilerParams(vmem_limit_bytes=58 * 2**20),
        cost_estimate=pl.CostEstimate(
            flops=2 * rows * ff * sk, bytes_accessed=6 * rows * ff, transcendentals=0
        ),
        name="update",
    )(stepped, sketched, left, right, self_sketch[0], mix_sketch[0], bkt, sgn, stream)
    return tuple(o[None] for o in outs)


def solution(mesh):
    split = P("blk", "fsdp", None)
    return jax.shard_map(
        body,
        mesh=mesh,
        in_specs=(P(("blk", "fsdp"), None), split, split, split, split, split, P(), P()),
        out_specs=(split, split, split, split),
        check_vma=False,
    )
```

```python
import jax
import jax.numpy as jnp
from jax import lax
from jax.experimental import pallas as pl
from jax.experimental.pallas import tpu as pltpu
from jax.sharding import PartitionSpec as P

MESH = pl.DeviceIdType.MESH
STEP_SIZE = 0.3
CONSENSUS = 0.5
CH = 256
LANES = 128
LEAD = 4
GAP = 2
PAIRS = 8
DEFER = 1
AHEAD = 4
FIRST_W = 2
OTHER = 4
LAG = 8
PIECES = 5
PARTS = 3
PUT = 3


def nt(a, b):
    return lax.dot_general(a, b, (((1,), (1,)), ((), ())), preferred_element_type=jnp.float32)


def nn(a, b):
    return jnp.dot(a, b, preferred_element_type=jnp.float32)


def chunk_row(ref, j):
    parts = CH // LANES
    return jnp.concatenate([ref[pl.ds(j * parts + p, 1), :] for p in range(parts)], axis=1)


def signed_table(bkt, sgn, j, sk):
    sign = (2 * chunk_row(sgn, j) - 1).astype(jnp.float32)
    hot = lax.broadcasted_iota(jnp.int32, (sk, CH), 0) == chunk_row(bkt, j)
    return sign, jnp.where(hot, jnp.broadcast_to(sign, (sk, CH)), 0.0).astype(jnp.bfloat16)


def gather_kernel(
    hid, res, cot, wgt, slf, bucket, bits,
    out_s, out_st, out_sk, out_left, out_right,
    buf, wv, cv, rv, sv, sacc, stepped, lhs, kacc, skf, sk_send, wpart, gsend, grecv, psend, precv, bkt, sgn,
    lsem, insem, sem1, sem2, sem3, sibsem, ssem, xsem, osem, gsem, wsem, psem,
):
    rows, ff = wgt.shape
    toks = hid.shape[0]
    nc = ff // CH
    slots = nc - PAIRS
    nb, nf = lax.axis_size("blk"), lax.axis_size("fsdp")
    sk = slf.shape[1]
    blk, me = lax.axis_index("blk"), lax.axis_index("fsdp")
    xh, y, core = me // 8, (me // 2) % 4, me % 2
    xo = 1 - xh

    def at(a, b):
        return a * 8 + (b % 4) * 2 + core

    sibling = me + 1 - 2 * core
    up, down, across = at(xh, y + 1), at(xh, y + 3), at(xo, y)
    ahead, behind = (blk + 1) % nb, (blk + nb - 1) % nb

    def chunk(i, half):
        paired = (slots + PAIRS - 1 - i) // slots
        return paired * (2 * i + half) + (1 - paired) * (i + PAIRS)

    def block(j, b):
        return buf.at[j, pl.ds(pl.multiple_of(b * toks, toks), toks), :]

    def span(j):
        return pl.ds(pl.multiple_of(j * CH, CH), CH)

    def load(j):
        return pltpu.make_async_copy(hid.at[:, span(j)], block(j, me), lsem.at[j])

    def send(i, j, b, to, recv, lane):
        pltpu.make_async_remote_copy(
            src_ref=block(j, b), dst_ref=block(j, b), send_sem=ssem.at[lane], recv_sem=recv.at[i],
            device_id=(blk, to), device_id_type=MESH,
        ).start()

    def hand(src, dst, recv, lane):
        pltpu.make_async_remote_copy(
            src_ref=src, dst_ref=dst, send_sem=ssem.at[lane], recv_sem=recv,
            device_id=(blk, across), device_id_type=MESH,
        ).start()

    def landed(ref, sem):
        pltpu.make_async_copy(ref, ref, sem).wait()

    def arrived(i, sem, blocks):
        landed(buf.at[i, pl.ds(0, blocks * toks), :], sem.at[i])

    def cross(i):
        other = chunk(i, xo)
        load(other).wait()
        send(i, other, me, across, sem1, 0)

    def own(i):
        j = chunk(i, xh)

        @pl.when(i < PAIRS)
        def _():
            load(j).wait()

        send(i, j, me, up, sem1, 0)
        send(i, j, me, down, sem1, 0)
        send(i, j, me, sibling, sibsem, 1)

    def forward(i, j, a, recv):
        half = toks // 2
        for b, to, start in ((at(a, y + 3), up, 0), (at(a, y + 1), down, half)):
            ref = buf.at[j, pl.ds(pl.multiple_of(b * toks + start, half), half), :]
            pltpu.make_async_remote_copy(
                src_ref=ref, dst_ref=ref, send_sem=ssem.at[0], recv_sem=recv.at[i],
                device_id=(blk, to), device_id_type=MESH,
            ).start()

    def second(i):
        arrived(i, sem1, 3)
        j = chunk(i, xh)
        forward(i, j, xh, sem2)
        send(i, j, across, up, sem2, 0)
        send(i, j, across, down, sem2, 0)
        send(i, j, up, sibling, sibsem, 1)
        send(i, j, down, sibling, sibsem, 1)
        send(i, j, across, sibling, sibsem, 1)

    def third(i):
        arrived(i, sem2, 3)
        j = chunk(i, xh)
        forward(i, j, xo, sem3)
        send(i, j, at(xh, y + 2), sibling, sibsem, 1)
        send(i, j, at(xo, y + 1), sibling, sibsem, 1)
        send(i, j, at(xo, y + 3), sibling, sibsem, 1)

    def fourth(i):
        arrived(i, sem3, 1)
        send(i, chunk(i, xh), at(xo, y + 2), sibling, sibsem, 1)

    def finish(j, gradient):
        new = wv[:, span(j)].astype(jnp.float32) - (STEP_SIZE * ff**-0.5) * gradient
        stepped[j] = new
        pltpu.make_async_copy(stepped.at[j], out_st.at[j], osem.at[0]).start()
        sign, table = signed_table(bkt, sgn, j, sk)
        high = new.astype(jnp.bfloat16)
        lhs[pl.ds(0, rows), :] = high
        lhs[pl.ds(rows, rows), :] = (new - high.astype(jnp.float32)).astype(jnp.bfloat16)
        lhs[pl.ds(2 * rows, 16), :] = jnp.broadcast_to(sign, (16, CH)).astype(jnp.bfloat16)
        kacc[...] += nt(lhs[...], table)

    mine, theirs = pl.ds(0, rows), pl.ds(rows, rows)

    def paired_step(k):
        arrived(k, sibsem, nf // 2)
        landed(wpart.at[k], wsem.at[k])
        j = chunk(k, xh)
        h = buf[j]
        both = nn(cv[...], h)
        gsend[k] = both[rows:].astype(jnp.bfloat16)
        hand(gsend.at[k], grecv.at[k], gsem.at[k], 4)
        finish(j, both[:rows])
        sacc[...] += nt(jnp.concatenate([wv[:, span(j)], wpart[k]], axis=0), h)

    def other_step(k):
        landed(grecv.at[k], gsem.at[k])
        finish(chunk(k, xo), grecv[k].astype(jnp.float32))

    def gradient_part(i):
        arrived(i, sibsem, nf // 2)
        j = chunk(i, xh)
        finish(j, nn(cv[mine, :], buf[j]))

    def product_part(i):
        j = chunk(i, xh)
        sacc[mine, :] += nt(wv[:, span(j)], buf[j])

    barrier = pltpu.get_barrier_semaphore()
    for to in (up, down, across, sibling):
        pl.semaphore_signal(barrier, inc=1, device_id=(blk, to), device_id_type=MESH)
    for to in (ahead, behind):
        pl.semaphore_signal(barrier, inc=1, device_id=(to, me), device_id_type=MESH)

    def start_load(j, c):
        load(j).start()
        return c

    lax.fori_loop(0, 2 * AHEAD, start_load, 0)
    ins = [(cot, cv.at[mine, :]), (wgt, wv), (bucket, bkt), (bits, sgn), (slf, sv), (res, rv)]
    ins = [pltpu.make_async_copy(a, b, insem.at[i]) for i, (a, b) in enumerate(ins)]
    ins[0].start()
    pl.semaphore_wait(barrier, 6)

    def lead(i, c):
        cross(i)
        own(i)
        return c

    def lead_cross(i, c):
        cross(i)
        return c

    lax.fori_loop(0, LEAD, lead, 0)
    for c in ins[1:]:
        c.start()
    lax.fori_loop(2 * AHEAD, nc, start_load, 0)
    lax.fori_loop(LEAD, AHEAD, lead_cross, 0)
    sacc[...] = jnp.zeros_like(sacc)
    kacc[...] = jnp.zeros_like(kacc)
    for c in ins:
        c.wait()

    last = 2 * GAP + 1
    strip = rows // PIECES
    first_sum = LAG + PAIRS

    def step(i, c):
        @pl.when(i + AHEAD < slots)
        def _():
            cross(i + AHEAD)

        @pl.when(i + LEAD < slots)
        def _():
            own(i + LEAD)

        @pl.when(i == 0)
        def _():
            for p in range(PIECES):
                hand(cv.at[pl.ds(p * strip, strip), :], cv.at[pl.ds(rows + p * strip, strip), :], psem.at[0], 2)

        @pl.when((i >= FIRST_W) & (i < FIRST_W + PAIRS // 2))
        def _():
            for q in range(2):
                k = 2 * (i - FIRST_W) + q
                hand(wv.at[:, span(chunk(k, xo))], wpart.at[k], wsem.at[k], 3)

        @pl.when(i == first_sum)
        def _():
            psend[...] = sacc[theirs, :].astype(jnp.bfloat16)
            for p in range(PIECES):
                there = pl.ds(p * strip, strip)
                hand(psend.at[there, :], precv.at[there, :], psem.at[1], 5)

        @pl.when(i < slots)
        def _():
            second(i)

        @pl.when((i >= GAP) & (i < slots + GAP))
        def _():
            third(i - GAP)

        @pl.when((i >= 2 * GAP) & (i < slots + 2 * GAP))
        def _():
            fourth(i - 2 * GAP)

        @pl.when(i >= PAIRS + last)
        def _():
            gradient_part(i - last)

        @pl.when(i == LAG)
        def _():
            landed(cv.at[theirs, :], psem.at[0])

        @pl.when((i >= LAG) & (i < first_sum))
        def _():
            paired_step(i - LAG)

        @pl.when((i >= (LAG + OTHER)) & (i < (LAG + OTHER) + PAIRS))
        def _():
            other_step(i - (LAG + OTHER))

        @pl.when(i >= PAIRS + last + DEFER)
        def _():
            product_part(i - last - DEFER)

        return c

    lax.fori_loop(0, slots + last, step, 0)

    sketched = (sk / ff) * (
        kacc[pl.ds(0, rows), :] + kacc[pl.ds(rows, rows), :] - kacc[pl.ds(2 * rows, 1), :] * sv[...]
    )
    sk_send[...] = sketched.astype(jnp.bfloat16)
    swaps = [
        pltpu.make_async_remote_copy(
            src_ref=sk_send, dst_ref=dst, send_sem=xsem.at[2 * i], recv_sem=xsem.at[2 * i + 1],
            device_id=(to, me), device_id_type=MESH,
        )
        for i, (dst, to) in enumerate(((out_left, ahead), (out_right, behind)))
    ]
    for c in swaps:
        c.start()
    skf[...] = sketched
    outs = [pltpu.make_async_copy(skf, out_sk, osem.at[1])]
    outs[0].start()

    def product_left(i, c):
        product_part(i)
        return c

    lax.fori_loop(slots - DEFER, slots, product_left, 0)
    landed(precv, psem.at[1])
    total = sacc[mine, :] + precv[...].astype(jnp.float32)
    rv[...] = (rv[...].astype(jnp.float32) + (ff**-0.5) * total).astype(jnp.bfloat16)
    outs.append(pltpu.make_async_copy(rv, out_s, osem.at[2]))
    outs[1].start()
    outs.append(pltpu.make_async_copy(stepped, out_st, osem.at[0]))
    for lane, blocks in ((0, 7), (1, 8)):
        landed(buf.at[pl.ds(0, slots), pl.ds(0, blocks * toks), :], ssem.at[lane])
    for i, ref in enumerate((cv.at[theirs, :], wpart, gsend, precv)):
        landed(ref, ssem.at[2 + i])
    for c in outs + swaps:
        c.wait()


def update_kernel(
    st, sketch, left, right, slf, mix, bucket, bits, stream,
    out_s, out_w, out_self, out_mix,
    stv, wv, av, lv, rv, sv, mv, dv, tv, bkt, sgn, insem, stsem, osem,
):
    nc = st.shape[0]
    sk = slf.shape[1]
    part = nc // PARTS

    def columns(ref, j):
        return ref.at[:, pl.ds(pl.multiple_of(j * CH, CH), PUT * CH)]

    def get(p):
        there = pl.ds(p * part, part)
        return pltpu.make_async_copy(st.at[there], stv.at[there], stsem.at[p])

    ins = [(left, lv), (right, rv), (sketch, av), (mix, mv), (slf, sv), (bucket, bkt), (bits, sgn), (stream, tv)]
    ins = [pltpu.make_async_copy(a, b, insem.at[i]) for i, (a, b) in enumerate(ins)]
    for c in ins:
        c.start()
    for p in range(PARTS):
        get(p).start()
    for c in ins[:7]:
        c.wait()
    new_self = sv[...] + av[...]
    new_mix = mv[...] + (lv[...].astype(jnp.float32) + av[...] + rv[...].astype(jnp.float32)) / 3.0
    dv[...] = (CONSENSUS * (new_mix - new_self)).astype(jnp.bfloat16)
    sv[...] = new_self
    mv[...] = new_mix
    ins[7].wait()
    outs = [(sv, out_self), (mv, out_mix), (tv, out_s)]
    outs = [pltpu.make_async_copy(a, b, osem.at[i]) for i, (a, b) in enumerate(outs)]
    for c in outs:
        c.start()

    def expand(p, c):
        get(p).wait()
        for q in range(part):
            j = p * part + q
            _, table = signed_table(bkt, sgn, j, sk)
            new = stv[j] + nn(dv[...], table)
            wv[:, pl.ds(pl.multiple_of(j * CH, CH), CH)] = new.astype(jnp.bfloat16)
            if q % PUT == PUT - 1:
                there = j - PUT + 1
                pltpu.make_async_copy(columns(wv, there), columns(out_w, there), osem.at[3]).start()
        return c

    lax.fori_loop(0, PARTS, expand, 0)
    outs.append(pltpu.make_async_copy(wv, out_w, osem.at[3]))
    for c in outs:
        c.wait()


def body(hidden, residual, cotangent, weight, self_sketch, mix_sketch, bucket, sign_bit):
    toks, ff = hidden.shape
    _, rows, whole = residual.shape
    sk = self_sketch.shape[2]
    nc = ff // CH
    f32, bf16 = jnp.float32, jnp.bfloat16
    anywhere = pl.BlockSpec(memory_space=pl.ANY)
    dma = pltpu.SemaphoreType.DMA
    shape = jax.ShapeDtypeStruct
    bkt, sgn = bucket.reshape(-1, LANES), sign_bit.reshape(-1, LANES)
    stream, stepped, sketched, left, right = pl.pallas_call(
        gather_kernel,
        out_shape=(
            shape((rows, whole), bf16),
            shape((nc, rows, CH), f32),
            shape((rows, sk), f32),
            shape((rows, sk), bf16),
            shape((rows, sk), bf16),
        ),
        in_specs=[anywhere] * 7,
        out_specs=(anywhere,) * 5,
        scratch_shapes=[
            pltpu.VMEM((nc, whole, CH), bf16),
            pltpu.VMEM((rows, ff), bf16),
            pltpu.VMEM((2 * rows, whole), bf16),
            pltpu.VMEM((rows, whole), bf16),
            pltpu.VMEM((rows, sk), f32),
            pltpu.VMEM((2 * rows, whole), f32),
            pltpu.VMEM((nc, rows, CH), f32),
            pltpu.VMEM((2 * rows + 16, CH), bf16),
            pltpu.VMEM((2 * rows + 16, sk), f32),
            pltpu.VMEM((rows, sk), f32),
            pltpu.VMEM((rows, sk), bf16),
            pltpu.VMEM((PAIRS, rows, CH), bf16),
            pltpu.VMEM((PAIRS, rows, CH), bf16),
            pltpu.VMEM((PAIRS, rows, CH), bf16),
            pltpu.VMEM((rows, whole), bf16),
            pltpu.VMEM((rows, whole), bf16),
            pltpu.VMEM(bkt.shape, jnp.int32),
            pltpu.VMEM(bkt.shape, jnp.int32),
            dma((nc,)), dma((6,)), dma((nc,)), dma((nc,)), dma((nc,)), dma((nc,)), dma((6,)), dma((4,)), dma((3,)),
            dma((PAIRS,)), dma((PAIRS,)), dma((2,)),
        ],
        compiler_params=pltpu.CompilerParams(
            collective_id=0, has_side_effects=True, vmem_limit_bytes=58 * 2**20
        ),
        cost_estimate=pl.CostEstimate(
            flops=2 * rows * ff * (2 * whole + 2 * sk), bytes_accessed=2 * (toks + 2 * rows) * ff, transcendentals=0
        ),
        name="gather_step_sketch",
    )(hidden, residual[0], cotangent[0], weight[0], self_sketch[0], bkt, sgn)
    outs = pl.pallas_call(
        update_kernel,
        out_shape=(
            shape((rows, whole), bf16),
            shape((rows, ff), bf16),
            shape((rows, sk), f32),
            shape((rows, sk), f32),
        ),
        in_specs=[anywhere] * 9,
        out_specs=(anywhere,) * 4,
        scratch_shapes=[
            pltpu.VMEM((nc, rows, CH), f32),
            pltpu.VMEM((rows, ff), bf16),
            pltpu.VMEM((rows, sk), f32),
            pltpu.VMEM((rows, sk), bf16),
            pltpu.VMEM((rows, sk), bf16),
            pltpu.VMEM((rows, sk), f32),
            pltpu.VMEM((rows, sk), f32),
            pltpu.VMEM((rows, sk), bf16),
            pltpu.VMEM((rows, whole), bf16),
            pltpu.VMEM(bkt.shape, jnp.int32),
            pltpu.VMEM(bkt.shape, jnp.int32),
            dma((8,)), dma((PARTS,)), dma((4,)),
        ],
        compiler_params=pltpu.CompilerParams(vmem_limit_bytes=58 * 2**20),
        cost_estimate=pl.CostEstimate(
            flops=2 * rows * ff * sk, bytes_accessed=6 * rows * ff, transcendentals=0
        ),
        name="update",
    )(stepped, sketched, left, right, self_sketch[0], mix_sketch[0], bkt, sgn, stream)
    return tuple(o[None] for o in outs)


def solution(mesh):
    split = P("blk", "fsdp", None)
    return jax.shard_map(
        body,
        mesh=mesh,
        in_specs=(P(("blk", "fsdp"), None), split, split, split, split, split, P(), P()),
        out_specs=(split, split, split, split),
        check_vma=False,
    )
```
